256 devices in a mesh: dp: 16 (over y, x), graph: 16 (over z, core).
Axes of the slice: x: 4, y: 4, z: 8, core: 2. Of those that a mesh axis runs over, the one named last changes fastest.
Arguments:
- edge_in: bfloat16 [262144, 512], P(('dp', 'graph')), may hold values from -6 to 6
- cotangent: bfloat16 [262144, 512], P(('dp', 'graph')), may hold values from -6 to 6
- weight_first: bfloat16 [512, 512], replicated, may hold values from -0.25 to 0.25
- weight_second: bfloat16 [512, 512], replicated, may hold values from -0.25 to 0.25
- weight_down: bfloat16 [64, 512], replicated, may hold values from -0.25 to 0.25
- weight_up: bfloat16 [64, 512], replicated, may hold values from -0.75 to 0.75
- coeffs: bfloat16 [6144, 128, 128], P(('dp', 'graph')), may hold values from -0.29882812 to 0.29882812
- tile_source: int32 [6144], P(('dp', 'graph')), may hold values from 0 to 127
- tile_target: int32 [6144], P(('dp', 'graph')), may hold values from 0 to 7
- tile_count: int32 [256], P(('dp', 'graph')), may hold values from 8 to 24, as said below
Outputs:
- edge_grad: bfloat16 [262144, 512], P(('dp', 'graph'))
- grad_first: float32 [512, 512], replicated
- grad_second: float32 [512, 512], replicated
- grad_down: float32 [64, 512], replicated
- grad_up: float32 [64, 512], replicated
The draws below stay inside these ranges and needn't reach their ends.
Inputs may be any that keep to these rules, and one draw needn't show every extreme that they name: `tile_count`: slots of a device at or beyond its count are padding: their sources, targets and coefficients are ignored. In every graph batch some device has exactly 24 live slots.
All inputs are finite; a program needn't handle non-finite values.
Results may differ from the reference program's by a relative error of at most 0.019.
Values may be sent and summed in bfloat16 or wider, within the bound.
A program may use at most 128 MiB of HBM per device.

```python
import jax
import jax.numpy as jnp
from jax import lax

D = 512
TW = 64
EDGES = 16384
TILES_DEV = 8
TILES_ALL = 128
SLOTS = 24
N_DP = 16
N_GRAPH = 16


def draw_tile_count(key, part):
    key = jax.random.fold_in(key, 7)
    count_key, full_key = jax.random.split(key)
    lowest = max(SLOTS // 3, 1)
    counts = jax.random.randint(count_key, (N_DP, N_GRAPH), lowest, SLOTS + 1)
    fullest = jax.random.randint(full_key, (N_DP, 1), 0, N_GRAPH)
    places = jnp.arange(N_GRAPH)[None, :]
    counts = jnp.where(places == fullest, SLOTS, counts)
    return counts.reshape(N_DP * N_GRAPH).astype(jnp.int32)


def set_ends(result, key, low, high):
    longest = result.shape.index(max(result.shape))
    spots = []
    for shift in (0, 1):
        where = [jax.random.randint(jax.random.fold_in(key, axis), (), 0, length) for axis, length in enumerate(result.shape)]
        where[longest] = (where[longest] + shift) % result.shape[longest]
        spots.append(tuple(where))
    return result.at[spots[0]].set(low).at[spots[1]].set(high)


def shard_levels(key, shape, shards, least, high):
    factor_of = 1.0
    for position, shards_of in shards:
        draws = jax.random.uniform(jax.random.fold_in(jax.random.fold_in(key, 6), position), (shards_of,), jnp.float32, least / len(shards), high / len(shards))
        factor_of = factor_of * jnp.repeat(jnp.exp(draws), shape[position] // shards_of).reshape((-1,) + (1,) * (len(shape) - 1 - position))
    return factor_of


def centred(key, shape, spread, reach, shards=(), kind=jnp.bfloat16):
    entries = spread * jax.random.normal(key, shape, jnp.float32)
    if shards:
        entries = entries * shard_levels(key, shape, shards, -0.22, 0.18)
    return jnp.clip(entries, -reach, reach).astype(kind)


def setup_inputs(seed: int = 0) -> dict:
    seeds = jax.random.split(jax.random.key(seed), 11)
    return {
        "edge_in": centred(seeds[0], (N_DP * EDGES, D), 1.0, 6.0, ((0, 256),)),
        "cotangent": centred(seeds[1], (N_DP * EDGES, D), 1.0, 6.0, ((0, 256),)),
        "weight_first": centred(seeds[2], (D, D), D ** -0.5, 0.25),
        "weight_second": centred(seeds[3], (D, D), D ** -0.5, 0.25),
        "weight_down": centred(seeds[4], (TW, D), D ** -0.5, 0.25),
        "weight_up": centred(seeds[5], (TW, D), TW ** -0.5, 0.75),
        "coeffs": centred(seeds[6], (N_DP * N_GRAPH * SLOTS, 128, 128), 0.05, 0.29882812, ((0, 256),)),
        "tile_source": set_ends(jax.random.randint(seeds[7], (N_DP * N_GRAPH * SLOTS,), 0, TILES_ALL), jax.random.fold_in(seeds[7], 1), 0, TILES_ALL - 1).astype(jnp.int32),
        "tile_target": set_ends(jax.random.randint(seeds[8], (N_DP * N_GRAPH * SLOTS,), 0, TILES_DEV), jax.random.fold_in(seeds[8], 1), 0, TILES_DEV - 1).astype(jnp.int32),
        "tile_count": draw_tile_count(jax.random.fold_in(seeds[10], 71), 0),
    }


def silu_grad(values):
    sigma = jax.nn.sigmoid(values)
    return sigma * (1.0 + values * (1.0 - sigma))

def batch_grads(pieces, weight_first, weight_second, weight_down, weight_up):
    edges, cotan, coeff_tiles, source_ids, target_ids, counts = pieces
    tiles_all = EDGES // 128
    pre_first = jnp.dot(edges, weight_first, preferred_element_type=jnp.float32)
    hidden_one = jax.nn.silu(pre_first).astype(jnp.bfloat16)
    pre_second = jnp.dot(hidden_one, weight_second, preferred_element_type=jnp.float32)
    states = (edges.astype(jnp.float32) + jax.nn.silu(pre_second)).astype(jnp.bfloat16)
    pre_down = jnp.dot(states, weight_down.T, preferred_element_type=jnp.float32)
    projected = jax.nn.silu(pre_down).astype(jnp.bfloat16)
    slot_index = jnp.arange(N_GRAPH * SLOTS, dtype=jnp.int32)
    owner_dev = slot_index // SLOTS
    usable = (slot_index % SLOTS < counts[owner_dev]).astype(jnp.float32)
    target_all = (owner_dev * (EDGES // N_GRAPH // 128) + target_ids).astype(jnp.int32)
    coeff_wide = coeff_tiles.astype(jnp.float32)
    source_rows = projected.reshape(tiles_all, 128, TW)[source_ids].astype(jnp.float32)
    contrib = jnp.einsum('kts,ksc->ktc', coeff_wide, source_rows) * usable[:, None, None]
    aggregate = jax.ops.segment_sum(contrib, target_all, num_segments=tiles_all)
    aggregate = aggregate.reshape(EDGES, TW).astype(jnp.bfloat16)
    pre_up = jnp.dot(aggregate, weight_up, preferred_element_type=jnp.float32)
    up_cot = (cotan.astype(jnp.float32) * silu_grad(pre_up)).astype(jnp.bfloat16)
    grad_up = jnp.dot(aggregate.T, up_cot, preferred_element_type=jnp.float32)
    agg_cot = jnp.dot(up_cot, weight_up.T, preferred_element_type=jnp.float32).astype(jnp.bfloat16)
    target_rows = agg_cot.reshape(tiles_all, 128, TW)[target_all].astype(jnp.float32)
    back = jnp.einsum('kts,ktc->ksc', coeff_wide, target_rows) * usable[:, None, None]
    source_cot = jax.ops.segment_sum(back, source_ids, num_segments=tiles_all).reshape(EDGES, TW)
    down_cot = (source_cot * silu_grad(pre_down)).astype(jnp.bfloat16)
    grad_down = jnp.dot(down_cot.T, states, preferred_element_type=jnp.float32)
    state_cot = cotan.astype(jnp.float32) + jnp.dot(down_cot, weight_down, preferred_element_type=jnp.float32)
    second_cot = (state_cot * silu_grad(pre_second)).astype(jnp.bfloat16)
    grad_second = jnp.dot(hidden_one.T, second_cot, preferred_element_type=jnp.float32)
    hidden_cot = jnp.dot(second_cot, weight_second.T, preferred_element_type=jnp.float32)
    first_cot = (hidden_cot * silu_grad(pre_first)).astype(jnp.bfloat16)
    grad_first = jnp.dot(edges.T, first_cot, preferred_element_type=jnp.float32)
    edge_grad = (state_cot + jnp.dot(first_cot, weight_first.T, preferred_element_type=jnp.float32)).astype(jnp.bfloat16)
    return (edge_grad, grad_first, grad_second, grad_down, grad_up)

def reference(edge_in, cotangent, weight_first, weight_second, weight_down, weight_up, coeffs, tile_source, tile_target, tile_count):
    pieces = (edge_in.reshape(N_DP, EDGES, D), cotangent.reshape(N_DP, EDGES, D), coeffs.reshape(N_DP, N_GRAPH * SLOTS, 128, 128), tile_source.reshape(N_DP, N_GRAPH * SLOTS), tile_target.reshape(N_DP, N_GRAPH * SLOTS), tile_count.reshape(N_DP, N_GRAPH))
    results = lax.map(lambda piece: batch_grads(piece, weight_first, weight_second, weight_down, weight_up), pieces)
    edge_grad = results[0].reshape(N_DP * EDGES, D)
    return (edge_grad, lax.optimization_barrier(jnp.sum(results[1], axis=0)), lax.optimization_barrier(jnp.sum(results[2], axis=0)), lax.optimization_barrier(jnp.sum(results[3], axis=0)), lax.optimization_barrier(jnp.sum(results[4], axis=0)))
```

```python
import functools

import jax
import jax.numpy as jnp
from jax import lax
from jax.experimental import pallas as pl
from jax.experimental.pallas import tpu as pltpu
from jax.sharding import PartitionSpec as P

F32 = jnp.float32
BF16 = jnp.bfloat16
MESH = pl.DeviceIdType.MESH
LAST = (((1,), (1,)), ((), ()))
FIRST = (((0,), (0,)), ((), ()))

NX, NY, NZ = 4, 4, 8
HALF = NZ // 2
D, TW = 512, 64
ROWS, TILE, TILES, SLOTS = 1024, 128, 8, 24
CH = 2
NCH = TILES // CH
RB = CH * TILE
EXTRA = TILE
WB = D + EXTRA


def sigmoid(v):
    return 0.5 * jnp.tanh(0.5 * v) + 0.5


def silu_grad(v):
    s = sigmoid(v)
    return s * (1.0 + v * (1.0 - s))


def dot(a, b):
    return jnp.dot(a, b, preferred_element_type=F32)


def dotg(a, b, dims):
    return lax.dot_general(a, b, dims, preferred_element_type=F32)


def rows_at(start, size, step):
    return pl.ds(pl.multiple_of(start, step), size)


class AllReduce:
    def __init__(self, place, loc, refs, sems):
        self.p = place
        self.loc = loc
        self.snd1, self.rcv1, self.acc, self.snd2, self.rcv2, self.acc3, self.snd3, self.rcv3, self.z4, self.fin = refs
        self.ssem, self.rsem = sems
        self.open = []

    def copy(self, src, dst, idx, dev):
        return pltpu.make_async_remote_copy(
            src_ref=src, dst_ref=dst, send_sem=self.ssem.at[idx], recv_sem=self.rsem.at[idx],
            device_id=dev, device_id_type=MESH,
        )

    def start(self, src, dst, idx, dev):
        c = self.copy(src, dst, idx, dev)
        c.start()
        self.open.append(c)

    def arrived(self, dst, idx):
        self.copy(dst, dst, idx, self.p.sib).wait_recv()

    def p1(self):
        p = self.p
        h = D // 2
        self.snd1[...] = self.loc[rows_at((1 - p.c) * h, h, h), :].astype(BF16)
        self.start(self.snd1, self.rcv1, 0, p.sib)

    def p2(self):
        p = self.p
        h, q = D // 2, D // 2 // NX
        self.arrived(self.rcv1, 0)
        acc = self.loc[rows_at(p.c * h, h, h), :] + self.rcv1[...].astype(F32)
        self.acc[...] = acc
        self.snd2[...] = acc.astype(BF16)
        for d in range(1, NX):
            xt = lax.rem(p.x + d, NX)
            self.start(self.snd2.at[rows_at(xt * q, q, q)], self.rcv2.at[p.x], d, (p.y * NX + xt, p.g))

    def p3(self):
        p = self.p
        q, r = D // 2 // NX, D // 2 // NX // NY
        acc = self.acc[rows_at(p.x * q, q, q), :]
        for d in range(1, NX):
            xs = lax.rem(p.x + NX - d, NX)
            self.arrived(self.rcv2.at[xs], d)
            acc = acc + self.rcv2[xs].astype(F32)
        self.acc3[...] = acc
        self.snd3[...] = acc.astype(BF16)
        for d in range(1, NY):
            yt = lax.rem(p.y + d, NY)
            self.start(self.snd3.at[rows_at(yt * r, r, r)], self.rcv3.at[p.y], 3 + d, (yt * NX + p.x, p.g))

    def p4(self):
        p = self.p
        r = D // 2 // NX // NY
        acc = self.acc3[rows_at(p.y * r, r, r), :]
        for d in range(1, NY):
            ys = lax.rem(p.y + NY - d, NY)
            self.arrived(self.rcv3.at[ys], 3 + d)
            acc = acc + self.rcv3[ys].astype(F32)
        self.z4[p.z] = acc.astype(BF16)
        for d in (4, 3, 5, 2, 6, 1, 7):
            zt = lax.rem(p.z + d, NZ)
            self.start(self.z4.at[p.z], self.z4.at[p.z], 6 + d, (p.dp, zt * 2 + p.c))

    def mine(self, start, size):
        return self.fin.at[rows_at(start, size, size)]

    def p5(self):
        p = self.p
        r = D // 2 // NX // NY
        for d in range(1, NZ):
            zs = lax.rem(p.z + NZ - d, NZ)
            self.arrived(self.z4.at[zs], 6 + d)
        acc = self.z4[0].astype(F32)
        for i in range(1, NZ):
            acc = acc + self.z4[i].astype(F32)
        base = (p.c * NX + p.x) * NY
        self.fin[rows_at((base + p.y) * r, r, r), :] = acc.astype(BF16)
        for d in range(1, NY):
            yt = lax.rem(p.y + d, NY)
            part = self.mine((base + p.y) * r, r)
            self.start(part, part, 13 + d, (yt * NX + p.x, p.g))

    def p6(self):
        p = self.p
        q, r = D // 2 // NX, D // 2 // NX // NY
        base = (p.c * NX + p.x) * NY
        for d in range(1, NY):
            ys = lax.rem(p.y + NY - d, NY)
            self.arrived(self.mine((base + ys) * r, r), 13 + d)
        part = self.mine((p.c * NX + p.x) * q, q)
        for d in range(1, NX):
            xt = lax.rem(p.x + d, NX)
            self.start(part, part, 16 + d, (p.y * NX + xt, p.g))

    def p7(self):
        p = self.p
        h, q = D // 2, D // 2 // NX
        for d in range(1, NX):
            xs = lax.rem(p.x + NX - d, NX)
            self.arrived(self.mine((p.c * NX + xs) * q, q), 16 + d)
        part = self.mine(p.c * h, h)
        self.start(part, part, 20, p.sib)

    def p8(self):
        h = D // 2
        self.arrived(self.mine((1 - self.p.c) * h, h), 20)

    def close(self):
        for c in self.open:
            c.wait_send()


class Place:
    def __init__(self):
        self.dp = lax.axis_index("dp")
        self.g = lax.axis_index("graph")
        self.y, self.x = lax.div(self.dp, NX), lax.rem(self.dp, NX)
        self.z, self.c = lax.div(self.g, 2), lax.rem(self.g, 2)
        self.sib = (self.dp, self.z * 2 + 1 - self.c)

    def zdev(self, off):
        return (self.dp, self.zat(off) * 2 + self.c)

    def zat(self, off):
        return lax.rem(self.z + off + NZ, NZ)

    def partners(self):
        out = [self.sib]
        out += [self.zdev(d) for d in range(1, NZ)]
        out += [(self.y * NX + lax.rem(self.x + d, NX), self.g) for d in range(1, NX)]
        out += [(lax.rem(self.y + d, NY) * NX + self.x, self.g) for d in range(1, NY)]
        return out


def kernel(
    ts, tt, tc, x_hbm, g_hbm, w1_hbm, w2_hbm, wd_hbm, wu_hbm, co_hbm,
    eg_hbm, a_hbm, b_hbm,
    x, g, w1, w2, wd, wu, co, in_sem,
    d1, d2, h1t, xt, states, pd, proj, ag_s, ag_r, as_s, as_r,
    sl, tl, prev_s, prev_t, last_t, idx,
    comb, agg, upcot, aggcot,
    sib_snd, sib_rcv, rs_snd, rs_rcv, rb_s, rb_r, rr_s, rr_r,
    downcot, sc, second, first, ga, gb, eg, eg_sem, out_sem,
    *ar,
):
    p = Place()
    loads = [
        pltpu.make_async_copy(s, t, in_sem.at[i])
        for i, (s, t) in enumerate(
            ((x_hbm, x), (w1_hbm, w1), (w2_hbm, w2), (wd_hbm, wd), (co_hbm, co), (wu_hbm, wu), (g_hbm, g))
        )
    ]
    for c in loads:
        c.start()
    barrier = pltpu.get_barrier_semaphore()
    partners = p.partners()
    for dev in partners:
        pl.semaphore_signal(barrier, inc=1, device_id=dev, device_id_type=MESH)
    pl.semaphore_wait(barrier, len(partners))
    opened = []

    def block(zi, core, ch, n=CH):
        return proj.at[pl.ds((zi * 2 + core) * TILES + ch * CH, n)]

    def ring(side, step, ch):
        b = block(p.zat(-step if side == 0 else step), p.c, ch)
        return pltpu.make_async_remote_copy(
            src_ref=b, dst_ref=b, send_sem=ag_s.at[side, step, ch], recv_sem=ag_r.at[side, step, ch],
            device_id=p.zdev(1 if side == 0 else -1), device_id_type=MESH,
        )

    def ring_arrival(side, step, ch):
        b = block(p.zat(-1 - step if side == 0 else 1 + step), p.c, ch)
        pltpu.make_async_remote_copy(
            src_ref=b, dst_ref=b, send_sem=ag_s.at[side, step, ch], recv_sem=ag_r.at[side, step, ch],
            device_id=p.sib, device_id_type=MESH,
        ).wait_recv()

    def share(off, ch, core):
        b = block(p.zat(off), core, ch)
        k = off % NZ
        return pltpu.make_async_remote_copy(
            src_ref=b, dst_ref=b, send_sem=as_s.at[k, ch], recv_sem=as_r.at[k, ch],
            device_id=p.sib, device_id_type=MESH,
        )

    for i in range(4):
        loads[i].wait()

    @pl.loop(0, NCH)
    def _(i):
        rows = rows_at(i * RB, RB, RB)
        m = x[rows, :]
        v1 = dot(m, w1[...])
        h = (v1 * sigmoid(v1)).astype(BF16)
        d1[rows, :] = v1
        v2 = dot(h, w2[...])
        st = (m.astype(F32) + v2 * sigmoid(v2)).astype(BF16)
        d2[rows, :] = v2
        first[rows, :] = h
        states[rows, :] = st
        vd = dotg(wd[...], st, LAST)
        pr = (vd * sigmoid(vd)).astype(BF16)
        for j in range(CH):
            pd[i * CH + j] = vd[:, j * TILE:(j + 1) * TILE]
            proj[p.g * TILES + i * CH + j] = pr[:, j * TILE:(j + 1) * TILE]
        ring(0, 0, i).start()
        ring(1, 0, i).start()
        share(0, i, p.c).start()

    count = tc[0]
    for k in range(SLOTS):
        live = k < count
        sl[k] = jnp.where(live, ts[k], -1)
        tl[k] = jnp.where(live, tt[k], -1)
    for k in range(SLOTS):
        a = jnp.int32(SLOTS)
        b = jnp.int32(SLOTS)
        for e in range(k):
            a = jnp.where(sl[e] == ts[k], e, a)
            b = jnp.where(tl[e] == tt[k], e, b)
        prev_s[k] = a
        prev_t[k] = b
    for j in range(TILES):
        a = jnp.int32(SLOTS)
        for k in range(SLOTS):
            a = jnp.where(tl[k] == j, k, a)
        last_t[j] = a

    def tables(lo, hi):
        @pl.loop(lo, hi)
        def _(j):
            a = jnp.int32(SLOTS)
            for k in range(SLOTS):
                a = jnp.where(sl[k] == j, k, a)
            idx[j] = a

    def side_work(i):
        rows = rows_at(i * RB, RB, RB)
        d1[rows, :] = silu_grad(d1[rows, :])
        d2[rows, :] = silu_grad(d2[rows, :])
        h1t[:, rows] = first[rows, :].T
        xt[:, rows] = x[rows, :].T

    comb[SLOTS] = jnp.zeros((TW, TILE), F32)

    for s in range(HALF):
        for ch in range(NCH):
            for side in (0, 1):
                lower = ch < NCH // 2
                mine = (side == 0) == lower
                if s == HALF - 1 and not mine:
                    continue
                ring_arrival(side, s, ch)
                if s + 1 < HALF - 1 or (s + 1 == HALF - 1 and mine):
                    ring(side, s + 1, ch).start()
                share(-1 - s if side == 0 else 1 + s, ch, p.c).start()
        if s < HALF:
            side_work(s)
            tables(s * 32, s * 32 + 32)

    for off in range(NZ):
        for ch in range(NCH):
            share(off, ch, 1 - p.c).wait_recv()

    loads[4].wait()
    for k in range(SLOTS):
        part = dotg(proj[ts[k]], co[k], LAST)
        comb[k] = part + comb[prev_t[k]]
    for j in range(TILES):
        agg[:, j * TILE:(j + 1) * TILE] = comb[last_t[j]].astype(BF16)

    loads[5].wait()
    loads[6].wait()

    @pl.loop(0, NCH)
    def _(i):
        rows = rows_at(i * RB, RB, RB)
        pu = dotg(agg[:, rows], wu[...], FIRST)
        uc = (g[rows, :].astype(F32) * silu_grad(pu)).astype(BF16)
        upcot[rows, :] = uc
        ac = dotg(wu[...], uc, LAST).astype(BF16)
        for j in range(CH):
            aggcot[i * CH + j] = ac[:, j * TILE:(j + 1) * TILE]

    for k in range(SLOTS):
        part = dot(aggcot[tt[k]], co[k])
        comb[k] = part + comb[prev_s[k]]

    def sib_copy(off):
        k = off % NZ
        return pltpu.make_async_remote_copy(
            src_ref=sib_snd.at[k], dst_ref=sib_rcv.at[k], send_sem=rb_s.at[k], recv_sem=rb_r.at[k],
            device_id=p.sib, device_id_type=MESH,
        )

    order = (4, 3, -3, 2, -2, 1, -1, 0)
    for off in order:
        base = (p.zat(off) * 2 + 1 - p.c) * TILES
        k = off % NZ

        @pl.loop(0, TILES)
        def _(j):
            sib_snd[k, j] = comb[idx[base + j]].astype(BF16)

        sib_copy(off).start()

    def red(side, step, ch):
        return pltpu.make_async_remote_copy(
            src_ref=rs_snd.at[side, step, pl.ds(ch * CH, CH)], dst_ref=rs_rcv.at[side, step, pl.ds(ch * CH, CH)],
            send_sem=rr_s.at[side, step, ch], recv_sem=rr_r.at[side, step, ch],
            device_id=p.zdev(1 if side == 0 else -1), device_id_type=MESH,
        )

    for s in range(HALF):
        for side in (0, 1):
            off = HALF - s if side == 0 else s - HALF
            base = (p.zat(off) * 2 + p.c) * TILES
            if s > 0 or side == 0:
                sib_copy(off).wait_recv()
            for ch in range(NCH):
                mine = (side == 0) == (ch < NCH // 2)
                if s == 0 and not mine:
                    continue
                more = s > 1 or (s == 1 and mine)
                if more:
                    red(side, s - 1, ch).wait_recv()
                for j in range(ch * CH, ch * CH + CH):
                    v = comb[idx[base + j]] + sib_rcv[off % NZ, j].astype(F32)
                    if more:
                        v = v + rs_rcv[side, s - 1, j].astype(F32)
                    rs_snd[side, s, j] = v.astype(BF16)
                red(side, s, ch).start()
        if s == 0:
            gu = dot(agg[...], upcot[...])
            for b in range(D // TILE):
                gb[b * TILE:b * TILE + TW, D:] = gu[:, b * TILE:(b + 1) * TILE]

    sib_copy(0).wait_recv()
    base = p.g * TILES
    for ch in range(NCH):
        red(0, HALF - 1, ch).wait_recv()
        red(1, HALF - 1, ch).wait_recv()
        for j in range(ch * CH, ch * CH + CH):
            v = comb[idx[base + j]] + sib_rcv[0, j].astype(F32)
            v = v + rs_rcv[0, HALF - 1, j].astype(F32) + rs_rcv[1, HALF - 1, j].astype(F32)
            downcot[:, j * TILE:(j + 1) * TILE] = (v * silu_grad(pd[j])).astype(BF16)

    @pl.loop(0, NCH)
    def _(i):
        rows = rows_at(i * RB, RB, RB)
        v = g[rows, :].astype(F32) + dotg(downcot[:, rows], wd[...], FIRST)
        sc[rows, :] = v
        second[rows, :] = (v * d2[rows, :]).astype(BF16)

    @pl.loop(0, D // 256)
    def _(i):
        rows = rows_at(i * 256, 256, 256)
        gb[rows, :D] = dot(h1t[rows, :], second[...])

    gd = dot(downcot[...], states[...])
    for b in range(D // TILE):
        gb[b * TILE + TW:(b + 1) * TILE, D:] = gd[:, b * TILE:(b + 1) * TILE]

    n = len(ar) // 2
    ar_a = AllReduce(p, ga, ar[:n - 2], ar[n - 2:n])
    ar_b = AllReduce(p, gb, ar[n:2 * n - 2], ar[2 * n - 2:])
    ar_b.p1()

    @pl.loop(0, NCH)
    def _(i):
        rows = rows_at(i * RB, RB, RB)
        v = dotg(second[rows, :], w2[...], LAST)
        first[rows, :] = (v * d1[rows, :]).astype(BF16)

    ar_b.p2()

    @pl.loop(0, D // 256)
    def _(i):
        rows = rows_at(i * 256, 256, 256)
        ga[rows, :] = dot(xt[rows, :], first[...])

    ar_a.p1()
    ar_b.p3()

    def eg_copy(i):
        rows = rows_at(i * RB, RB, RB)
        return pltpu.make_async_copy(eg.at[rows, :], eg_hbm.at[rows, :], eg_sem.at[i])

    def edges(lo, hi):
        @pl.loop(lo, hi)
        def _(i):
            rows = rows_at(i * RB, RB, RB)
            v = sc[rows, :] + dotg(first[rows, :], w1[...], LAST)
            eg[rows, :] = v.astype(BF16)
            eg_copy(i).start()

    ar_a.p2()
    ar_b.p4()
    edges(0, NCH // 2)
    ar_a.p3()
    ar_b.p5()
    edges(NCH // 2, NCH)
    ar_a.p4()
    ar_b.p6()
    ar_a.p5()
    ar_b.p7()
    ar_a.p6()
    ar_b.p8()
    ob = pltpu.make_async_copy(ar_b.fin, b_hbm, out_sem.at[1])
    ob.start()
    ar_a.p7()
    ar_a.p8()
    oa = pltpu.make_async_copy(ar_a.fin, a_hbm, out_sem.at[0])
    oa.start()

    for ch in range(NCH):
        for side in (0, 1):
            for s in range(HALF):
                mine = (side == 0) == (ch < NCH // 2)
                if s < HALF - 1 or mine:
                    ring(side, s, ch).wait_send()
                if s > 0 or mine:
                    red(side, s, ch).wait_send()
        for off in range(NZ):
            share(off, ch, p.c).wait_send()
        eg_copy(ch).wait()
    for off in range(NZ):
        sib_copy(off).wait_send()
    ar_a.close()
    ar_b.close()
    ob.wait()
    oa.wait()


def ar_scratch(w):
    h, q, r = D // 2, D // 2 // NX, D // 2 // NX // NY
    return [
        pltpu.VMEM((h, w), BF16), pltpu.VMEM((h, w), BF16), pltpu.VMEM((h, w), F32), pltpu.VMEM((h, w), BF16),
        pltpu.VMEM((NX, q, w), BF16), pltpu.VMEM((q, w), F32), pltpu.VMEM((q, w), BF16),
        pltpu.VMEM((NY, r, w), BF16), pltpu.VMEM((NZ, r, w), BF16), pltpu.VMEM((D, w), BF16),
        pltpu.SemaphoreType.DMA((21,)), pltpu.SemaphoreType.DMA((21,)),
    ]


def on_device(
    edge_in, cotangent, weight_first, weight_second, weight_down, weight_up,
    coeffs, tile_source, tile_target, tile_count,
):
    V, S = pltpu.VMEM, pltpu.SMEM
    dma = pltpu.SemaphoreType.DMA
    scratch = [
        V((ROWS, D), BF16), V((ROWS, D), BF16), V((D, D), BF16), V((D, D), BF16),
        V((TW, D), BF16), V((TW, D), BF16), V((SLOTS, TILE, TILE), BF16), dma((7,)),
        V((ROWS, D), F32), V((ROWS, D), F32), V((D, ROWS), BF16), V((D, ROWS), BF16),
        V((ROWS, D), BF16), V((TILES, TW, TILE), F32), V((2 * NZ * TILES, TW, TILE), BF16),
        dma((2, HALF, NCH)), dma((2, HALF, NCH)), dma((NZ, NCH)), dma((NZ, NCH)),
        S((SLOTS,), jnp.int32), S((SLOTS,), jnp.int32), S((SLOTS,), jnp.int32), S((SLOTS,), jnp.int32),
        S((TILES,), jnp.int32), S((2 * NZ * TILES,), jnp.int32),
        V((SLOTS + 1, TW, TILE), F32), V((TW, ROWS), BF16), V((ROWS, D), BF16), V((TILES, TW, TILE), BF16),
        V((NZ, TILES, TW, TILE), BF16), V((NZ, TILES, TW, TILE), BF16),
        V((2, HALF, TILES, TW, TILE), BF16), V((2, HALF, TILES, TW, TILE), BF16),
        dma((NZ,)), dma((NZ,)), dma((2, HALF, NCH)), dma((2, HALF, NCH)),
        V((TW, ROWS), BF16), V((ROWS, D), F32), V((ROWS, D), BF16), V((ROWS, D), BF16),
        V((D, D), F32), V((D, WB), F32), V((ROWS, D), BF16), dma((NCH,)), dma((2,)),
    ] + ar_scratch(D) + ar_scratch(WB)
    hbm = pl.BlockSpec(memory_space=pl.ANY)
    smem = pl.BlockSpec(memory_space=pltpu.SMEM)
    edge_grad, a, b = pl.pallas_call(
        kernel,
        out_shape=(
            jax.ShapeDtypeStruct((ROWS, D), BF16),
            jax.ShapeDtypeStruct((D, D), BF16),
            jax.ShapeDtypeStruct((D, WB), BF16),
        ),
        in_specs=[smem] * 3 + [hbm] * 7,
        out_specs=(hbm,) * 3,
        scratch_shapes=scratch,
        compiler_params=pltpu.CompilerParams(
            collective_id=0, has_side_effects=True, vmem_limit_bytes=56 * 1024 * 1024
        ),
        cost_estimate=pl.CostEstimate(flops=7_400_000_000, bytes_accessed=8_000_000, transcendentals=2_000_000),
    )(
        tile_source, tile_target, tile_count, edge_in, cotangent, weight_first, weight_second,
        weight_down, weight_up, coeffs,
    )
    extra = b[:, D:].reshape(D // TILE, 2, TW, TILE).transpose(1, 2, 0, 3).reshape(2, TW, D).astype(F32)
    return (edge_grad, a.astype(F32), b[:, :D].astype(F32), extra[1], extra[0])


def solution(mesh):
    return jax.shard_map(
        on_device,
        mesh=mesh,
        in_specs=(
            P(("dp", "graph"), None), P(("dp", "graph"), None), P(), P(), P(), P(),
            P(("dp", "graph"), None, None), P(("dp", "graph")), P(("dp", "graph")), P(("dp", "graph")),
        ),
        out_specs=(P(("dp", "graph"), None), P(), P(), P(), P()),
        check_vma=False,
    )
```

```python
import jax
import jax.numpy as jnp
from jax import lax
from jax.experimental import pallas as pl
from jax.experimental.pallas import tpu as pltpu
from jax.sharding import PartitionSpec as P

F32 = jnp.float32
BF16 = jnp.bfloat16
MESH = pl.DeviceIdType.MESH
LAST = (((1,), (1,)), ((), ()))
FIRST = (((0,), (0,)), ((), ()))

NX, NY, NZ = 4, 4, 8
HALF = NZ // 2
D, TW = 512, 64
ROWS, TILE, TILES, SLOTS = 1024, 128, 8, 24
CH = 2
NCH = TILES // CH
RB = CH * TILE
EXTRA = TILE
WB = D + EXTRA
N_DP = NX * NY
PIECE = D // 2 // N_DP
FAR_FIRST = sorted(range(1, N_DP), key=lambda e: (-(min(e // NX, NY - e // NX) + min(e % NX, NX - e % NX)), e))


def sigmoid(v):
    return 0.5 * jnp.tanh(0.5 * v) + 0.5


def silu_grad(v):
    s = sigmoid(v)
    return s * (1.0 + v * (1.0 - s))


def dot(a, b):
    return jnp.dot(a, b, preferred_element_type=F32)


def dotg(a, b, dims):
    return lax.dot_general(a, b, dims, preferred_element_type=F32)


def rows_at(start, size, step):
    return pl.ds(pl.multiple_of(start, step), size)


class AllReduce:
    def __init__(self, place, refs, sems):
        self.p = place
        self.snd1, self.rcv1, self.acc, self.snd2, self.rcv2, self.zs, self.fin = refs
        self.ssem, self.rsem = sems
        self.open = []

    def copy(self, src, dst, idx, dev):
        return pltpu.make_async_remote_copy(
            src_ref=src, dst_ref=dst, send_sem=self.ssem.at[idx], recv_sem=self.rsem.at[idx],
            device_id=dev, device_id_type=MESH,
        )

    def start(self, src, dst, idx, dev):
        c = self.copy(src, dst, idx, dev)
        c.start()
        self.open.append(c)

    def arrived(self, dst, idx):
        self.copy(dst, dst, idx, self.p.sib).wait_recv()

    def to_sibling(self):
        self.start(self.snd1, self.rcv1, 0, self.p.sib)

    def to_plane(self):
        p = self.p
        self.arrived(self.rcv1, 0)
        acc = self.acc[...] + self.rcv1[...].astype(F32)
        self.acc[...] = acc
        self.snd2[...] = acc.astype(BF16)
        for e in FAR_FIRST:
            to = p.dpat(e)
            self.start(self.snd2.at[rows_at(to * PIECE, PIECE, PIECE)], self.rcv2.at[p.dp], e, (to, p.g))

    def to_column(self):
        p = self.p
        acc = self.acc[rows_at(p.dp * PIECE, PIECE, PIECE), :]
        for e in FAR_FIRST[::-1]:
            frm = p.dpat(-e)
            self.arrived(self.rcv2.at[frm], e)
            acc = acc + self.rcv2[frm].astype(F32)
        self.zs[p.z] = acc.astype(BF16)
        for d in (4, 3, 5, 2, 6, 1, 7):
            self.start(self.zs.at[p.z], self.zs.at[p.z], 15 + d, p.zdev(d))

    def part(self, core, first, n):
        return self.fin.at[rows_at((core * N_DP + first) * PIECE, n * PIECE, n * PIECE)]

    def plane_back(self):
        p = self.p
        for d in (1, 7, 2, 6, 3, 5, 4):
            self.arrived(self.zs.at[p.zat(-d)], 15 + d)
        acc = self.zs[0].astype(F32)
        for i in range(1, NZ):
            acc = acc + self.zs[i].astype(F32)
        self.fin[rows_at((p.c * N_DP + p.dp) * PIECE, PIECE, PIECE), :] = acc.astype(BF16)
        mine = self.part(p.c, p.dp, 1)
        for e in FAR_FIRST:
            self.start(mine, mine, 22 + e, (p.dpat(e), p.g))

    def sibling_back(self):
        p = self.p
        for dy in (0, 1, 3, 2):
            for dx in (1, 3, 2, 0):
                e = dy * NX + dx
                if e:
                    self.arrived(self.part(p.c, p.dpat(-e), 1), 22 + e)
            ys = lax.rem(p.y + NY - dy, NY)
            group = self.part(p.c, ys * NX, NX)
            self.start(group, group, 38 + dy, p.sib)

    def end(self):
        p = self.p
        for dy in (0, 1, 3, 2):
            ys = lax.rem(p.y + NY - dy, NY)
            self.arrived(self.part(1 - p.c, ys * NX, NX), 38 + dy)

    def close(self):
        for c in self.open:
            c.wait_send()


class Place:
    def __init__(self):
        self.dp = lax.axis_index("dp")
        self.g = lax.axis_index("graph")
        self.y, self.x = lax.div(self.dp, NX), lax.rem(self.dp, NX)
        self.z, self.c = lax.div(self.g, 2), lax.rem(self.g, 2)
        self.sib = (self.dp, self.z * 2 + 1 - self.c)

    def zdev(self, off):
        return (self.dp, self.zat(off) * 2 + self.c)

    def zat(self, off):
        return lax.rem(self.z + off + NZ, NZ)

    def dpat(self, e):
        sign = 1 if e >= 0 else -1
        dy, dx = abs(e) // NX * sign, abs(e) % NX * sign
        return lax.rem(self.y + dy + NY, NY) * NX + lax.rem(self.x + dx + NX, NX)

    def partners(self):
        out = [self.sib]
        out += [self.zdev(d) for d in range(1, NZ)]
        out += [(self.dpat(e), self.g) for e in range(1, N_DP)]
        return out


def kernel(
    ts_hbm, tt_hbm, tc_hbm, x_hbm, g_hbm, w1_hbm, w2_hbm, wd_hbm, wu_hbm, co_hbm,
    eg_hbm, a_hbm, b_hbm,
    ts, tt, tc, x, g, w1, w2, wd, wu, co, in_sem,
    d1, d2, h1t, xt, states, pd, proj, ag_s, ag_r, as_s, as_r,
    sl, tl, prev_s, prev_t, last_t, idx,
    comb, agg, upcot, aggcot,
    sib_snd, sib_rcv, rs_snd, rs_rcv, rb_s, rb_r, rr_s, rr_r,
    downcot, sc, second, first, gx, eg, eg_sem, out_sem,
    *ar,
):
    p = Place()
    barrier = pltpu.get_barrier_semaphore()
    partners = p.partners()
    for dev in partners:
        pl.semaphore_signal(barrier, inc=1, device_id=dev, device_id_type=MESH)
    head, tail = pl.ds(0, RB), pl.ds(RB, ROWS - RB)
    pairs = (
        (x_hbm.at[head], x.at[head]), (w1_hbm, w1), (w2_hbm, w2), (wd_hbm, wd), (x_hbm.at[tail], x.at[tail]),
        (ts_hbm, ts), (tt_hbm, tt), (tc_hbm, tc), (co_hbm, co), (wu_hbm, wu), (g_hbm, g),
    )
    loads = [pltpu.make_async_copy(s, t, in_sem.at[i]) for i, (s, t) in enumerate(pairs)]
    for c in loads:
        c.start()

    def block(zi, core, ch, n=CH):
        return proj.at[pl.ds((zi * 2 + core) * TILES + ch * CH, n)]

    def ring(side, step, ch):
        b = block(p.zat(-step if side == 0 else step), p.c, ch)
        return pltpu.make_async_remote_copy(
            src_ref=b, dst_ref=b, send_sem=ag_s.at[side, step, ch], recv_sem=ag_r.at[side, step, ch],
            device_id=p.zdev(1 if side == 0 else -1), device_id_type=MESH,
        )

    def ring_arrival(side, step, ch):
        b = block(p.zat(-1 - step if side == 0 else 1 + step), p.c, ch)
        pltpu.make_async_remote_copy(
            src_ref=b, dst_ref=b, send_sem=ag_s.at[side, step, ch], recv_sem=ag_r.at[side, step, ch],
            device_id=p.sib, device_id_type=MESH,
        ).wait_recv()

    def share(off, ch, core):
        b = block(p.zat(off), core, ch)
        k = off % NZ
        return pltpu.make_async_remote_copy(
            src_ref=b, dst_ref=b, send_sem=as_s.at[k, ch], recv_sem=as_r.at[k, ch],
            device_id=p.sib, device_id_type=MESH,
        )

    def forward(i):
        rows = pl.ds(i * RB, RB) if isinstance(i, int) else rows_at(i * RB, RB, RB)
        m = x[rows, :]
        v1 = dot(m, w1[...])
        h = (v1 * sigmoid(v1)).astype(BF16)
        d1[rows, :] = v1
        v2 = dot(h, w2[...])
        st = (m.astype(F32) + v2 * sigmoid(v2)).astype(BF16)
        d2[rows, :] = v2
        first[rows, :] = h
        states[rows, :] = st
        vd = dotg(wd[...], st, LAST)
        pr = (vd * sigmoid(vd)).astype(BF16)
        for j in range(CH):
            pd[i * CH + j] = vd[:, j * TILE:(j + 1) * TILE]
            proj[p.g * TILES + i * CH + j] = pr[:, j * TILE:(j + 1) * TILE]

    def send_own(i):
        ring(0, 0, i).start()
        ring(1, 0, i).start()
        share(0, i, p.c).start()

    for i in range(4):
        loads[i].wait()
    forward(0)
    pl.semaphore_wait(barrier, len(partners))
    send_own(0)
    loads[4].wait()

    @pl.loop(1, NCH)
    def _(i):
        forward(i)
        send_own(i)

    for i in (5, 6, 7):
        loads[i].wait()

    count = tc[0]
    for k in range(SLOTS):
        live = k < count
        sl[k] = jnp.where(live, ts[k], -1)
        tl[k] = jnp.where(live, tt[k], -1)
    for k in range(SLOTS):
        a = jnp.int32(SLOTS)
        b = jnp.int32(SLOTS)
        for e in range(k):
            a = jnp.where(sl[e] == ts[k], e, a)
            b = jnp.where(tl[e] == tt[k], e, b)
        prev_s[k] = a
        prev_t[k] = b
    for j in range(TILES):
        a = jnp.int32(SLOTS)
        for k in range(SLOTS):
            a = jnp.where(tl[k] == j, k, a)
        last_t[j] = a

    def tables(lo, hi):
        @pl.loop(lo, hi)
        def _(j):
            a = jnp.int32(SLOTS)
            for k in range(SLOTS):
                a = jnp.where(sl[k] == j, k, a)
            idx[j] = a

    def side_work(u):
        n = ROWS // (HALF * NCH)
        rows = pl.ds(u * n, n)
        d1[rows, :] = silu_grad(d1[rows, :])
        d2[rows, :] = silu_grad(d2[rows, :])
        tables(u * 2 * NZ * TILES // (HALF * NCH), (u + 1) * 2 * NZ * TILES // (HALF * NCH))
        if u % 2 == 0:
            rows = pl.ds(u * n, 2 * n)
            h1t[:, rows] = first[rows, :].T
            xt[:, rows] = x[rows, :].T

    comb[SLOTS] = jnp.zeros((TW, TILE), F32)

    for s in range(HALF):
        for ch in range(NCH):
            side_work(s * NCH + ch)
            for side in (0, 1):
                mine = (side == 0) == (ch < NCH // 2)
                if s == HALF - 1 and not mine:
                    continue
                ring_arrival(side, s, ch)
                if s + 1 < HALF - 1 or (s + 1 == HALF - 1 and mine):
                    ring(side, s + 1, ch).start()
                share(-1 - s if side == 0 else 1 + s, ch, p.c).start()

    for off in range(NZ):
        for ch in range(NCH):
            share(off, ch, 1 - p.c).wait_recv()

    loads[8].wait()
    for k in range(SLOTS):
        part = dotg(proj[ts[k]], co[k], LAST)
        comb[k] = part + comb[prev_t[k]]
    for j in range(TILES):
        agg[:, j * TILE:(j + 1) * TILE] = comb[last_t[j]].astype(BF16)

    loads[9].wait()
    loads[10].wait()

    @pl.loop(0, NCH)
    def _(i):
        rows = rows_at(i * RB, RB, RB)
        pu = dotg(agg[:, rows], wu[...], FIRST)
        uc = (g[rows, :].astype(F32) * silu_grad(pu)).astype(BF16)
        upcot[rows, :] = uc
        ac = dotg(wu[...], uc, LAST).astype(BF16)
        for j in range(CH):
            aggcot[i * CH + j] = ac[:, j * TILE:(j + 1) * TILE]

    for k in range(SLOTS):
        part = dot(aggcot[tt[k]], co[k])
        comb[k] = part + comb[prev_s[k]]

    def sib_copy(off):
        k = off % NZ
        return pltpu.make_async_remote_copy(
            src_ref=sib_snd.at[k], dst_ref=sib_rcv.at[k], send_sem=rb_s.at[k], recv_sem=rb_r.at[k],
            device_id=p.sib, device_id_type=MESH,
        )

    def red(side, step, ch):
        return pltpu.make_async_remote_copy(
            src_ref=rs_snd.at[side, step, pl.ds(ch * CH, CH)], dst_ref=rs_rcv.at[side, step, pl.ds(ch * CH, CH)],
            send_sem=rr_s.at[side, step, ch], recv_sem=rr_r.at[side, step, ch],
            device_id=p.zdev(1 if side == 0 else -1), device_id_type=MESH,
        )

    def for_sibling(off):
        base = (p.zat(off) * 2 + 1 - p.c) * TILES
        for j in range(TILES):
            sib_snd[off % NZ, j] = comb[idx[base + j]].astype(BF16)
        sib_copy(off).start()

    for_sibling(HALF)
    for s in range(HALF):
        if s + 1 < HALF:
            for_sibling(HALF - 1 - s)
            for_sibling(s + 1 - HALF)
        else:
            for_sibling(0)
        sib_copy(HALF - s).wait_recv()
        if s > 0:
            sib_copy(s - HALF).wait_recv()
        for ch in range(NCH):
            for side in (0, 1):
                off = HALF - s if side == 0 else s - HALF
                base = (p.zat(off) * 2 + p.c) * TILES
                mine = (side == 0) == (ch < NCH // 2)
                if s == 0 and not mine:
                    continue
                more = s > 1 or (s == 1 and mine)
                if more:
                    red(side, s - 1, ch).wait_recv()
                for j in range(ch * CH, ch * CH + CH):
                    v = comb[idx[base + j]] + sib_rcv[off % NZ, j].astype(F32)
                    if more:
                        v = v + rs_rcv[side, s - 1, j].astype(F32)
                    rs_snd[side, s, j] = v.astype(BF16)
                red(side, s, ch).start()
        if s == HALF - 1:
            gu = dot(agg[...], upcot[...])
            for b in range(D // TILE):
                gx[b * TILE:b * TILE + TW, :] = gu[:, b * TILE:(b + 1) * TILE]

    sib_copy(0).wait_recv()
    base = p.g * TILES
    for ch in range(NCH):
        red(0, HALF - 1, ch).wait_recv()
        red(1, HALF - 1, ch).wait_recv()
        for j in range(ch * CH, ch * CH + CH):
            v = comb[idx[base + j]] + sib_rcv[0, j].astype(F32)
            v = v + rs_rcv[0, HALF - 1, j].astype(F32) + rs_rcv[1, HALF - 1, j].astype(F32)
            downcot[:, j * TILE:(j + 1) * TILE] = (v * silu_grad(pd[j])).astype(BF16)

    @pl.loop(0, NCH)
    def _(i):
        rows = rows_at(i * RB, RB, RB)
        v = g[rows, :].astype(F32) + dotg(downcot[:, rows], wd[...], FIRST)
        sc[rows, :] = v
        second[rows, :] = (v * d2[rows, :]).astype(BF16)

    gd = dot(downcot[...], states[...])
    for b in range(D // TILE):
        gx[b * TILE + TW:(b + 1) * TILE, :] = gd[:, b * TILE:(b + 1) * TILE]

    n = len(ar) // 2
    ar_a = AllReduce(p, ar[:n - 2], ar[n - 2:n])
    ar_b = AllReduce(p, ar[n:2 * n - 2], ar[2 * n - 2:])
    h = D // 2
    theirs, own = rows_at((1 - p.c) * h, h, h), rows_at(p.c * h, h, h)
    ar_b.snd1[:, :D] = dot(h1t[theirs, :], second[...]).astype(BF16)
    ar_b.snd1[:, D:] = gx[theirs, :].astype(BF16)
    ar_b.to_sibling()
    ar_b.acc[:, :D] = dot(h1t[own, :], second[...])
    ar_b.acc[:, D:] = gx[own, :]

    @pl.loop(0, NCH)
    def _(i):
        rows = rows_at(i * RB, RB, RB)
        v = dotg(second[rows, :], w2[...], LAST)
        first[rows, :] = (v * d1[rows, :]).astype(BF16)

    ar_b.to_plane()
    ar_a.snd1[...] = dot(xt[theirs, :], first[...]).astype(BF16)
    ar_a.to_sibling()
    ar_a.acc[...] = dot(xt[own, :], first[...])

    def eg_copy(i):
        rows = rows_at(i * RB, RB, RB)
        return pltpu.make_async_copy(eg.at[rows, :], eg_hbm.at[rows, :], eg_sem.at[i])

    def edges(lo, hi):
        @pl.loop(lo, hi)
        def _(i):
            rows = rows_at(i * RB, RB, RB)
            v = sc[rows, :] + dotg(first[rows, :], w1[...], LAST)
            eg[rows, :] = v.astype(BF16)
            eg_copy(i).start()

    edges(0, 1)
    ar_a.to_plane()
    edges(1, 2)
    ar_b.to_column()
    edges(2, NCH)
    ar_a.to_column()
    ar_b.plane_back()
    ar_a.plane_back()
    ar_b.sibling_back()
    ar_a.sibling_back()
    ar_b.end()
    ob = pltpu.make_async_copy(ar_b.fin, b_hbm, out_sem.at[1])
    ob.start()
    ar_a.end()
    oa = pltpu.make_async_copy(ar_a.fin, a_hbm, out_sem.at[0])
    oa.start()

    for ch in range(NCH):
        for side in (0, 1):
            for s in range(HALF):
                mine = (side == 0) == (ch < NCH // 2)
                if s < HALF - 1 or mine:
                    ring(side, s, ch).wait_send()
                if s > 0 or mine:
                    red(side, s, ch).wait_send()
        for off in range(NZ):
            share(off, ch, p.c).wait_send()
        eg_copy(ch).wait()
    for off in range(NZ):
        sib_copy(off).wait_send()
    ar_a.close()
    ar_b.close()
    ob.wait()
    oa.wait()


def ar_scratch(w):
    h = D // 2
    return [
        pltpu.VMEM((h, w), BF16), pltpu.VMEM((h, w), BF16), pltpu.VMEM((h, w), F32), pltpu.VMEM((h, w), BF16),
        pltpu.VMEM((N_DP, PIECE, w), BF16), pltpu.VMEM((NZ, PIECE, w), BF16), pltpu.VMEM((D, w), BF16),
        pltpu.SemaphoreType.DMA((42,)), pltpu.SemaphoreType.DMA((42,)),
    ]


def widen(e_in, a_in, b_in, e_out, a_out, b_out, d_out, u_out, e, a, b, fa, fb, fd, fu, in_sem, out_sem, e_sem):
    n = 4
    parts = [pl.ds(i * (ROWS // n), ROWS // n) for i in range(n)]
    la = pltpu.make_async_copy(a_in, a, in_sem.at[0])
    lb = pltpu.make_async_copy(b_in, b, in_sem.at[1])
    le = [pltpu.make_async_copy(e_in.at[r], e.at[r], in_sem.at[2 + i]) for i, r in enumerate(parts)]
    se = [pltpu.make_async_copy(e.at[r], e_out.at[r], e_sem.at[i]) for i, r in enumerate(parts)]
    outs = [
        pltpu.make_async_copy(s, t, out_sem.at[i])
        for i, (s, t) in enumerate(((fa, a_out), (fb, b_out), (fd, d_out), (fu, u_out)))
    ]
    for c in [la, lb] + le:
        c.start()
    la.wait()
    fa[...] = a[...].astype(F32)
    outs[0].start()
    lb.wait()
    fb[...] = b[:, :D].astype(F32)
    outs[1].start()
    for k in range(D // TILE):
        cols = pl.ds(k * TILE, TILE)
        fu[:, cols] = b[k * TILE:k * TILE + TW, D:].astype(F32)
        fd[:, cols] = b[k * TILE + TW:(k + 1) * TILE, D:].astype(F32)
    outs[2].start()
    outs[3].start()
    for i in range(n):
        le[i].wait()
        se[i].start()
    for c in se + outs:
        c.wait()


def on_device(
    edge_in, cotangent, weight_first, weight_second, weight_down, weight_up,
    coeffs, tile_source, tile_target, tile_count,
):
    V, S = pltpu.VMEM, pltpu.SMEM
    dma = pltpu.SemaphoreType.DMA
    scratch = [
        S((SLOTS,), jnp.int32), S((SLOTS,), jnp.int32), S((1,), jnp.int32),
        V((ROWS, D), BF16), V((ROWS, D), BF16), V((D, D), BF16), V((D, D), BF16),
        V((TW, D), BF16), V((TW, D), BF16), V((SLOTS, TILE, TILE), BF16), dma((11,)),
        V((ROWS, D), F32), V((ROWS, D), F32), V((D, ROWS), BF16), V((D, ROWS), BF16),
        V((ROWS, D), BF16), V((TILES, TW, TILE), F32), V((2 * NZ * TILES, TW, TILE), BF16),
        dma((2, HALF, NCH)), dma((2, HALF, NCH)), dma((NZ, NCH)), dma((NZ, NCH)),
        S((SLOTS,), jnp.int32), S((SLOTS,), jnp.int32), S((SLOTS,), jnp.int32), S((SLOTS,), jnp.int32),
        S((TILES,), jnp.int32), S((2 * NZ * TILES,), jnp.int32),
        V((SLOTS + 1, TW, TILE), F32), V((TW, ROWS), BF16), V((ROWS, D), BF16), V((TILES, TW, TILE), BF16),
        V((NZ, TILES, TW, TILE), BF16), V((NZ, TILES, TW, TILE), BF16),
        V((2, HALF, TILES, TW, TILE), BF16), V((2, HALF, TILES, TW, TILE), BF16),
        dma((NZ,)), dma((NZ,)), dma((2, HALF, NCH)), dma((2, HALF, NCH)),
        V((TW, ROWS), BF16), V((ROWS, D), F32), V((ROWS, D), BF16), V((ROWS, D), BF16),
        V((D, EXTRA), F32), V((ROWS, D), BF16), dma((NCH,)), dma((2,)),
    ] + ar_scratch(D) + ar_scratch(WB)
    hbm = pl.BlockSpec(memory_space=pl.ANY)
    edge_grad, a, b = pl.pallas_call(
        kernel,
        out_shape=(
            jax.ShapeDtypeStruct((ROWS, D), BF16),
            jax.ShapeDtypeStruct((D, D), BF16),
            jax.ShapeDtypeStruct((D, WB), BF16),
        ),
        in_specs=[hbm] * 10,
        out_specs=(hbm,) * 3,
        scratch_shapes=scratch,
        compiler_params=pltpu.CompilerParams(
            collective_id=0, has_side_effects=True, vmem_limit_bytes=56 * 1024 * 1024
        ),
        cost_estimate=pl.CostEstimate(flops=7_400_000_000, bytes_accessed=8_000_000, transcendentals=2_000_000),
    )(
        tile_source, tile_target, tile_count, edge_in, cotangent, weight_first, weight_second,
        weight_down, weight_up, coeffs,
    )
    grad = jax.ShapeDtypeStruct((D, D), F32)
    small = jax.ShapeDtypeStruct((TW, D), F32)
    return pl.pallas_call(
        widen,
        out_shape=(jax.ShapeDtypeStruct((ROWS, D), BF16), grad, grad, small, small),
        in_specs=[hbm] * 3,
        out_specs=(hbm,) * 5,
        scratch_shapes=[
            V((ROWS, D), BF16), V((D, D), BF16), V((D, WB), BF16),
            V((D, D), F32), V((D, D), F32), V((TW, D), F32), V((TW, D), F32),
            dma((6,)), dma((4,)), dma((4,)),
        ],
        compiler_params=pltpu.CompilerParams(vmem_limit_bytes=60 * 1024 * 1024),
        cost_estimate=pl.CostEstimate(flops=600_000, bytes_accessed=5_700_000, transcendentals=0),
    )(edge_grad, a, b)


def solution(mesh):
    return jax.shard_map(
        on_device,
        mesh=mesh,
        in_specs=(
            P(("dp", "graph"), None), P(("dp", "graph"), None), P(), P(), P(), P(),
            P(("dp", "graph"), None, None), P(("dp", "graph")), P(("dp", "graph")), P(("dp", "graph")),
        ),
        out_specs=(P(("dp", "graph"), None), P(), P(), P(), P()),
        check_vma=False,
    )
```

```python
import jax
import jax.numpy as jnp
from jax import lax
from jax.experimental import pallas as pl
from jax.experimental.pallas import tpu as pltpu
from jax.sharding import PartitionSpec as P

F32 = jnp.float32
BF16 = jnp.bfloat16
MESH = pl.DeviceIdType.MESH
LAST = (((1,), (1,)), ((), ()))
FIRST = (((0,), (0,)), ((), ()))

NX, NY, NZ = 4, 4, 8
HALF = NZ // 2
D, TW = 512, 64
ROWS, TILE, TILES, SLOTS = 1024, 128, 8, 24
CH = 2
NCH = TILES // CH
RB = CH * TILE
EXTRA = TILE
WB = D + EXTRA
N_DP = NX * NY
PIECE = D // 2 // N_DP
FAR_FIRST = sorted(range(1, N_DP), key=lambda e: (-(min(e // NX, NY - e // NX) + min(e % NX, NX - e % NX)), e))


def sigmoid(v):
    return 0.5 * jnp.tanh(0.5 * v) + 0.5


def silu_grad(v):
    s = sigmoid(v)
    return s * (1.0 + v * (1.0 - s))


def dot(a, b):
    return jnp.dot(a, b, preferred_element_type=F32)


def dotg(a, b, dims):
    return lax.dot_general(a, b, dims, preferred_element_type=F32)


def rows_at(start, size, step):
    return pl.ds(pl.multiple_of(start, step), size)


class AllReduce:
    def __init__(self, place, refs, sems):
        self.p = place
        self.snd1, self.rcv1, self.acc, self.snd2, self.rcv2, self.zs, self.fin = refs
        self.ssem, self.rsem = sems
        self.open = []

    def copy(self, src, dst, idx, dev):
        return pltpu.make_async_remote_copy(
            src_ref=src, dst_ref=dst, send_sem=self.ssem.at[idx], recv_sem=self.rsem.at[idx],
            device_id=dev, device_id_type=MESH,
        )

    def start(self, src, dst, idx, dev):
        c = self.copy(src, dst, idx, dev)
        c.start()
        self.open.append(c)

    def arrived(self, dst, idx):
        self.copy(dst, dst, idx, self.p.sib).wait_recv()

    def to_sibling(self):
        self.start(self.snd1, self.rcv1, 0, self.p.sib)

    def to_plane(self):
        p = self.p
        self.arrived(self.rcv1, 0)
        acc = self.acc[...] + self.rcv1[...].astype(F32)
        self.acc[...] = acc
        self.snd2[...] = acc.astype(BF16)
        for e in FAR_FIRST:
            to = p.dpat(e)
            self.start(self.snd2.at[rows_at(to * PIECE, PIECE, PIECE)], self.rcv2.at[p.dp], e, (to, p.g))

    def to_column(self):
        p = self.p
        acc = self.acc[rows_at(p.dp * PIECE, PIECE, PIECE), :]
        for e in FAR_FIRST[::-1]:
            frm = p.dpat(-e)
            self.arrived(self.rcv2.at[frm], e)
            acc = acc + self.rcv2[frm].astype(F32)
        self.zs[p.z] = acc.astype(BF16)
        for d in (4, 3, 5, 2, 6, 1, 7):
            self.start(self.zs.at[p.z], self.zs.at[p.z], 15 + d, p.zdev(d))

    def part(self, core, first, n):
        return self.fin.at[rows_at((core * N_DP + first) * PIECE, n * PIECE, n * PIECE)]

    def plane_back(self):
        p = self.p
        for d in (1, 7, 2, 6, 3, 5, 4):
            self.arrived(self.zs.at[p.zat(-d)], 15 + d)
        acc = self.zs[0].astype(F32)
        for i in range(1, NZ):
            acc = acc + self.zs[i].astype(F32)
        self.fin[rows_at((p.c * N_DP + p.dp) * PIECE, PIECE, PIECE), :] = acc.astype(BF16)
        mine = self.part(p.c, p.dp, 1)
        for e in FAR_FIRST:
            self.start(mine, mine, 22 + e, (p.dpat(e), p.g))

    def sibling_back(self):
        p = self.p
        for dy in (0, 1, 3, 2):
            for dx in (1, 3, 2, 0):
                e = dy * NX + dx
                if e:
                    self.arrived(self.part(p.c, p.dpat(-e), 1), 22 + e)
            ys = lax.rem(p.y + NY - dy, NY)
            group = self.part(p.c, ys * NX, NX)
            self.start(group, group, 38 + dy, p.sib)

    def end(self):
        p = self.p
        for dy in (0, 1, 3, 2):
            ys = lax.rem(p.y + NY - dy, NY)
            self.arrived(self.part(1 - p.c, ys * NX, NX), 38 + dy)

    def close(self, keep=0):
        n = len(self.open) - keep
        for c in self.open[:n]:
            c.wait_send()
        self.open = self.open[n:]


class Place:
    def __init__(self):
        self.dp = lax.axis_index("dp")
        self.g = lax.axis_index("graph")
        self.y, self.x = lax.div(self.dp, NX), lax.rem(self.dp, NX)
        self.z, self.c = lax.div(self.g, 2), lax.rem(self.g, 2)
        self.sib = (self.dp, self.z * 2 + 1 - self.c)

    def zdev(self, off):
        return (self.dp, self.zat(off) * 2 + self.c)

    def zat(self, off):
        return lax.rem(self.z + off + NZ, NZ)

    def dpat(self, e):
        sign = 1 if e >= 0 else -1
        dy, dx = abs(e) // NX * sign, abs(e) % NX * sign
        return lax.rem(self.y + dy + NY, NY) * NX + lax.rem(self.x + dx + NX, NX)

    def partners(self):
        out = [self.sib]
        out += [self.zdev(d) for d in range(1, NZ)]
        out += [(self.dpat(e), self.g) for e in range(1, N_DP)]
        return out


def kernel(
    ts_hbm, tt_hbm, tc_hbm, x_hbm, g_hbm, w1_hbm, w2_hbm, wd_hbm, wu_hbm, co_hbm,
    eg_hbm, a_hbm, b_hbm,
    ts, tt, tc, x, g, w1, w2, wd, wu, co, in_sem,
    d1, d2, h1t, xt, states, pd, proj, ag_s, ag_r, as_s, as_r,
    tab_v, tab,
    comb, agg, upcot, aggcot,
    sib_snd, sib_rcv, rs_snd, rs_rcv, rb_s, rb_r, rr_s, rr_r,
    downcot, sc, second, first, gx, eg, eg_sem, out_sem,
    *ar,
):
    p = Place()
    barrier = pltpu.get_barrier_semaphore()
    partners = p.partners()
    for dev in partners:
        pl.semaphore_signal(barrier, inc=1, device_id=dev, device_id_type=MESH)
    head, tail = pl.ds(0, RB), pl.ds(RB, ROWS - RB)
    pairs = (
        (x_hbm.at[head], x.at[head]), (w1_hbm, w1), (w2_hbm, w2), (wd_hbm, wd), (x_hbm.at[tail], x.at[tail]),
        (ts_hbm, ts), (tt_hbm, tt), (tc_hbm, tc), (co_hbm, co), (wu_hbm, wu), (g_hbm, g),
    )
    loads = [pltpu.make_async_copy(s, t, in_sem.at[i]) for i, (s, t) in enumerate(pairs)]
    for c in loads:
        c.start()

    def block(zi, core, ch, n=CH):
        return proj.at[pl.ds((zi * 2 + core) * TILES + ch * CH, n)]

    def ring(side, step, ch):
        back, on = (step, 1) if step < HALF - 1 else (HALF - 2, 2)
        b = block(p.zat(-back if side == 0 else back), p.c, ch)
        return pltpu.make_async_remote_copy(
            src_ref=b, dst_ref=b, send_sem=ag_s.at[side, step, ch], recv_sem=ag_r.at[side, step, ch],
            device_id=p.zdev(on if side == 0 else -on), device_id_type=MESH,
        )

    def ring_arrival(side, step, ch):
        b = block(p.zat(-1 - step if side == 0 else 1 + step), p.c, ch)
        pltpu.make_async_remote_copy(
            src_ref=b, dst_ref=b, send_sem=ag_s.at[side, step, ch], recv_sem=ag_r.at[side, step, ch],
            device_id=p.sib, device_id_type=MESH,
        ).wait_recv()

    def share(off, ch, core):
        b = block(p.zat(off), core, ch)
        k = off % NZ
        return pltpu.make_async_remote_copy(
            src_ref=b, dst_ref=b, send_sem=as_s.at[k, ch], recv_sem=as_r.at[k, ch],
            device_id=p.sib, device_id_type=MESH,
        )

    def forward(i):
        rows = pl.ds(i * RB, RB) if isinstance(i, int) else rows_at(i * RB, RB, RB)
        m = x[rows, :]
        v1 = dot(m, w1[...])
        h = (v1 * sigmoid(v1)).astype(BF16)
        d1[rows, :] = v1
        v2 = dot(h, w2[...])
        st = (m.astype(F32) + v2 * sigmoid(v2)).astype(BF16)
        d2[rows, :] = v2
        first[rows, :] = h
        states[rows, :] = st
        vd = dotg(wd[...], st, LAST)
        pr = (vd * sigmoid(vd)).astype(BF16)
        for j in range(CH):
            pd[i * CH + j] = vd[:, j * TILE:(j + 1) * TILE]
            proj[p.g * TILES + i * CH + j] = pr[:, j * TILE:(j + 1) * TILE]

    def send_own(i):
        ring(0, 0, i).start()
        ring(1, 0, i).start()
        share(0, i, p.c).start()

    for i in range(4):
        loads[i].wait()
    forward(0)
    pl.semaphore_wait(barrier, len(partners))
    send_own(0)
    loads[4].wait()

    @pl.loop(1, NCH)
    def _(i):
        forward(i)
        send_own(i)

    for i in (5, 6, 7):
        loads[i].wait()

    count = tc[0]
    lane = lax.broadcasted_iota(jnp.int32, (1, TILE), 1)
    none = jnp.full((1, TILE), SLOTS, jnp.int32)
    sv = tv = jnp.zeros((1, TILE), jnp.int32)
    for k in range(SLOTS):
        sv = jnp.where(lane == k, ts[k], sv)
        tv = jnp.where(lane == k, tt[k], tv)
    before_s = before_t = final_s = final_t = none
    for k in range(SLOTS):
        live = k < count
        sk = jnp.where(live, ts[k], -1)
        tk = jnp.where(live, tt[k], -1)
        later = lane > k
        before_s = jnp.where(later & (sv == sk), k, before_s)
        before_t = jnp.where(later & (tv == tk), k, before_t)
        final_s = jnp.where(lane == sk, k, final_s)
        final_t = jnp.where(lane == tk, k, final_t)
    for i, v in enumerate((final_s, before_s, before_t, final_t, none, none, none, none)):
        tab_v[i:i + 1, :] = v
    to_scalar = pltpu.make_async_copy(tab_v, tab, in_sem.at[11])
    to_scalar.start()

    def side_work(u):
        n = ROWS // (HALF * NCH)
        rows = pl.ds(u * n, n)
        d1[rows, :] = silu_grad(d1[rows, :])
        d2[rows, :] = silu_grad(d2[rows, :])
        if u * n % TILE == 0:
            rows = pl.ds(u * n, TILE)
            h1t[:, rows] = first[rows, :].T
            xt[:, rows] = x[rows, :].T

    comb[SLOTS] = jnp.zeros((TW, TILE), F32)

    for s in range(HALF):
        for ch in range(NCH):
            side_work(s * NCH + ch)
            for side in (0, 1):
                mine = (side == 0) == (ch < NCH // 2)
                if s == HALF - 1 and not mine:
                    continue
                ring_arrival(side, s, ch)
                if s == HALF - 3 and mine:
                    ring(side, HALF - 1, ch).start()
                if s < HALF - 2:
                    ring(side, s + 1, ch).start()
                share(-1 - s if side == 0 else 1 + s, ch, p.c).start()

    for off in range(NZ):
        for ch in range(NCH):
            share(off, ch, 1 - p.c).wait_recv()

    loads[8].wait()
    to_scalar.wait()
    for k in range(SLOTS):
        part = dotg(proj[ts[k]], co[k], LAST)
        comb[k] = part + comb[tab[2, k]]
    for j in range(TILES):
        agg[:, j * TILE:(j + 1) * TILE] = comb[tab[3, j]].astype(BF16)

    loads[9].wait()
    loads[10].wait()

    @pl.loop(0, NCH)
    def _(i):
        rows = rows_at(i * RB, RB, RB)
        pu = dotg(agg[:, rows], wu[...], FIRST)
        uc = (g[rows, :].astype(F32) * silu_grad(pu)).astype(BF16)
        upcot[rows, :] = uc
        ac = dotg(wu[...], uc, LAST).astype(BF16)
        for j in range(CH):
            aggcot[i * CH + j] = ac[:, j * TILE:(j + 1) * TILE]

    for k in range(SLOTS):
        part = dot(aggcot[tt[k]], co[k])
        comb[k] = part + comb[tab[1, k]]

    def sib_copy(off):
        k = off % NZ
        return pltpu.make_async_remote_copy(
            src_ref=sib_snd.at[k], dst_ref=sib_rcv.at[k], send_sem=rb_s.at[k], recv_sem=rb_r.at[k],
            device_id=p.sib, device_id_type=MESH,
        )

    def red(side, step, ch):
        on = 1 if step else 2
        return pltpu.make_async_remote_copy(
            src_ref=rs_snd.at[side, step, pl.ds(ch * CH, CH)], dst_ref=rs_rcv.at[side, step, pl.ds(ch * CH, CH)],
            send_sem=rr_s.at[side, step, ch], recv_sem=rr_r.at[side, step, ch],
            device_id=p.zdev(on if side == 0 else -on), device_id_type=MESH,
        )

    def for_sibling(off):
        base = (p.zat(off) * 2 + 1 - p.c) * TILES
        for j in range(TILES):
            sib_snd[off % NZ, j] = comb[tab[0, base + j]].astype(BF16)
        sib_copy(off).start()

    for_sibling(HALF)
    for s in range(HALF):
        if s + 1 < HALF:
            for_sibling(HALF - 1 - s)
            for_sibling(s + 1 - HALF)
        else:
            for_sibling(0)
        sib_copy(HALF - s).wait_recv()
        if s > 0:
            sib_copy(s - HALF).wait_recv()
        for q in range(NCH):
            for side in (0, 1):
                ch = (q + NCH // 2) % NCH if side == 0 else q
                off = HALF - s if side == 0 else s - HALF
                base = (p.zat(off) * 2 + p.c) * TILES
                mine = (side == 0) == (ch < NCH // 2)
                if s == 0 and not mine:
                    continue
                joins = [s - 1] if s > 1 else []
                if s == 2 and mine:
                    joins.append(0)
                for e in joins:
                    red(side, e, ch).wait_recv()
                for j in range(ch * CH, ch * CH + CH):
                    v = comb[tab[0, base + j]] + sib_rcv[off % NZ, j].astype(F32)
                    for e in joins:
                        v = v + rs_rcv[side, e, j].astype(F32)
                    rs_snd[side, s, j] = v.astype(BF16)
                red(side, s, ch).start()
        if s == HALF - 1:
            gu = dot(agg[...], upcot[...])
            for b in range(D // TILE):
                gx[b * TILE:b * TILE + TW, :] = gu[:, b * TILE:(b + 1) * TILE]

    sib_copy(0).wait_recv()
    base = p.g * TILES
    for ch in range(NCH):
        red(0, HALF - 1, ch).wait_recv()
        red(1, HALF - 1, ch).wait_recv()
        for j in range(ch * CH, ch * CH + CH):
            v = comb[tab[0, base + j]] + sib_rcv[0, j].astype(F32)
            v = v + rs_rcv[0, HALF - 1, j].astype(F32) + rs_rcv[1, HALF - 1, j].astype(F32)
            downcot[:, j * TILE:(j + 1) * TILE] = (v * silu_grad(pd[j])).astype(BF16)

    @pl.loop(0, NCH)
    def _(i):
        rows = rows_at(i * RB, RB, RB)
        v = g[rows, :].astype(F32) + dotg(downcot[:, rows], wd[...], FIRST)
        sc[rows, :] = v
        second[rows, :] = (v * d2[rows, :]).astype(BF16)

    gd = dot(downcot[...], states[...])
    for b in range(D // TILE):
        gx[b * TILE + TW:(b + 1) * TILE, :] = gd[:, b * TILE:(b + 1) * TILE]

    n = len(ar) // 2
    ar_a = AllReduce(p, ar[:n - 2], ar[n - 2:n])
    ar_b = AllReduce(p, ar[n:2 * n - 2], ar[2 * n - 2:])
    h = D // 2
    theirs, own = rows_at((1 - p.c) * h, h, h), rows_at(p.c * h, h, h)
    ar_b.snd1[:, :D] = dot(h1t[theirs, :], second[...]).astype(BF16)
    ar_b.snd1[:, D:] = gx[theirs, :].astype(BF16)
    ar_b.to_sibling()
    ar_b.acc[:, :D] = dot(h1t[own, :], second[...])
    ar_b.acc[:, D:] = gx[own, :]

    @pl.loop(0, NCH)
    def _(i):
        rows = rows_at(i * RB, RB, RB)
        v = dotg(second[rows, :], w2[...], LAST)
        first[rows, :] = (v * d1[rows, :]).astype(BF16)

    ar_b.to_plane()
    ar_a.snd1[...] = dot(xt[theirs, :], first[...]).astype(BF16)
    ar_a.to_sibling()
    ar_a.acc[...] = dot(xt[own, :], first[...])

    def eg_copy(i):
        rows = rows_at(i * RB, RB, RB)
        return pltpu.make_async_copy(eg.at[rows, :], eg_hbm.at[rows, :], eg_sem.at[i])

    def edges(lo, hi):
        @pl.loop(lo, hi)
        def _(i):
            rows = rows_at(i * RB, RB, RB)
            v = sc[rows, :] + dotg(first[rows, :], w1[...], LAST)
            eg[rows, :] = v.astype(BF16)
            eg_copy(i).start()

    edges(0, 2)
    ar_b.to_column()
    ar_a.to_plane()
    edges(2, NCH)

    for ch in range(NCH):
        for side in (0, 1):
            for s in range(HALF):
                mine = (side == 0) == (ch < NCH // 2)
                if s < HALF - 1 or mine:
                    ring(side, s, ch).wait_send()
                if s > 0 or mine:
                    red(side, s, ch).wait_send()
        for off in range(NZ):
            share(off, ch, p.c).wait_send()
    for off in range(NZ):
        sib_copy(off).wait_send()

    ar_b.plane_back()
    ar_a.to_column()
    ar_b.close(N_DP - 1)
    ar_a.close(NZ - 1)
    ar_a.plane_back()
    ar_b.close()
    ar_a.close(N_DP - 1)
    ar_b.sibling_back()
    ar_a.sibling_back()
    ar_b.end()
    ob = pltpu.make_async_copy(ar_b.fin, b_hbm, out_sem.at[1])
    ob.start()
    ar_a.end()
    oa = pltpu.make_async_copy(ar_a.fin, a_hbm, out_sem.at[0])
    oa.start()

    for i in range(NCH):
        eg_copy(i).wait()
    ar_b.close()
    ar_a.close()
    ob.wait()
    oa.wait()


def ar_scratch(w):
    h = D // 2
    return [
        pltpu.VMEM((h, w), BF16), pltpu.VMEM((h, w), BF16), pltpu.VMEM((h, w), F32), pltpu.VMEM((h, w), BF16),
        pltpu.VMEM((N_DP, PIECE, w), BF16), pltpu.VMEM((NZ, PIECE, w), BF16), pltpu.VMEM((D, w), BF16),
        pltpu.SemaphoreType.DMA((42,)), pltpu.SemaphoreType.DMA((42,)),
    ]


def widen(e_in, a_in, b_in, e_out, a_out, b_out, d_out, u_out, e, a, b, fa, fb, fd, fu, in_sem, out_sem, e_sem):
    n = 4
    parts = [pl.ds(i * (ROWS // n), ROWS // n) for i in range(n)]
    la = pltpu.make_async_copy(a_in, a, in_sem.at[0])
    lb = pltpu.make_async_copy(b_in, b, in_sem.at[1])
    le = [pltpu.make_async_copy(e_in.at[r], e.at[r], in_sem.at[2 + i]) for i, r in enumerate(parts)]
    se = [pltpu.make_async_copy(e.at[r], e_out.at[r], e_sem.at[i]) for i, r in enumerate(parts)]
    outs = [
        pltpu.make_async_copy(s, t, out_sem.at[i])
        for i, (s, t) in enumerate(((fa, a_out), (fb, b_out), (fd, d_out), (fu, u_out)))
    ]
    for c in [la, lb] + le:
        c.start()
    la.wait()
    fa[...] = a[...].astype(F32)
    outs[0].start()
    lb.wait()
    fb[...] = b[:, :D].astype(F32)
    outs[1].start()
    for k in range(D // TILE):
        cols = pl.ds(k * TILE, TILE)
        fu[:, cols] = b[k * TILE:k * TILE + TW, D:].astype(F32)
        fd[:, cols] = b[k * TILE + TW:(k + 1) * TILE, D:].astype(F32)
    outs[2].start()
    outs[3].start()
    for i in range(n):
        le[i].wait()
        se[i].start()
    for c in se + outs:
        c.wait()


def on_device(
    edge_in, cotangent, weight_first, weight_second, weight_down, weight_up,
    coeffs, tile_source, tile_target, tile_count,
):
    V, S = pltpu.VMEM, pltpu.SMEM
    dma = pltpu.SemaphoreType.DMA
    scratch = [
        S((SLOTS,), jnp.int32), S((SLOTS,), jnp.int32), S((1,), jnp.int32),
        V((ROWS, D), BF16), V((ROWS, D), BF16), V((D, D), BF16), V((D, D), BF16),
        V((TW, D), BF16), V((TW, D), BF16), V((SLOTS, TILE, TILE), BF16), dma((12,)),
        V((ROWS, D), F32), V((ROWS, D), F32), V((D, ROWS), BF16), V((D, ROWS), BF16),
        V((ROWS, D), BF16), V((TILES, TW, TILE), F32), V((2 * NZ * TILES, TW, TILE), BF16),
        dma((2, HALF, NCH)), dma((2, HALF, NCH)), dma((NZ, NCH)), dma((NZ, NCH)),
        V((8, TILE), jnp.int32), S((8, TILE), jnp.int32),
        V((SLOTS + 1, TW, TILE), F32), V((TW, ROWS), BF16), V((ROWS, D), BF16), V((TILES, TW, TILE), BF16),
        V((NZ, TILES, TW, TILE), BF16), V((NZ, TILES, TW, TILE), BF16),
        V((2, HALF, TILES, TW, TILE), BF16), V((2, HALF, TILES, TW, TILE), BF16),
        dma((NZ,)), dma((NZ,)), dma((2, HALF, NCH)), dma((2, HALF, NCH)),
        V((TW, ROWS), BF16), V((ROWS, D), F32), V((ROWS, D), BF16), V((ROWS, D), BF16),
        V((D, EXTRA), F32), V((ROWS, D), BF16), dma((NCH,)), dma((2,)),
    ] + ar_scratch(D) + ar_scratch(WB)
    hbm = pl.BlockSpec(memory_space=pl.ANY)
    edge_grad, a, b = pl.pallas_call(
        kernel,
        out_shape=(
            jax.ShapeDtypeStruct((ROWS, D), BF16),
            jax.ShapeDtypeStruct((D, D), BF16),
            jax.ShapeDtypeStruct((D, WB), BF16),
        ),
        in_specs=[hbm] * 10,
        out_specs=(hbm,) * 3,
        scratch_shapes=scratch,
        compiler_params=pltpu.CompilerParams(
            collective_id=0, has_side_effects=True, vmem_limit_bytes=56 * 1024 * 1024
        ),
        cost_estimate=pl.CostEstimate(flops=7_400_000_000, bytes_accessed=8_000_000, transcendentals=2_000_000),
    )(
        tile_source, tile_target, tile_count, edge_in, cotangent, weight_first, weight_second,
        weight_down, weight_up, coeffs,
    )
    grad = jax.ShapeDtypeStruct((D, D), F32)
    small = jax.ShapeDtypeStruct((TW, D), F32)
    return pl.pallas_call(
        widen,
        out_shape=(jax.ShapeDtypeStruct((ROWS, D), BF16), grad, grad, small, small),
        in_specs=[hbm] * 3,
        out_specs=(hbm,) * 5,
        scratch_shapes=[
            V((ROWS, D), BF16), V((D, D), BF16), V((D, WB), BF16),
            V((D, D), F32), V((D, D), F32), V((TW, D), F32), V((TW, D), F32),
            dma((6,)), dma((4,)), dma((4,)),
        ],
        compiler_params=pltpu.CompilerParams(vmem_limit_bytes=60 * 1024 * 1024),
        cost_estimate=pl.CostEstimate(flops=600_000, bytes_accessed=5_700_000, transcendentals=0),
    )(edge_grad, a, b)


def solution(mesh):
    return jax.shard_map(
        on_device,
        mesh=mesh,
        in_specs=(
            P(("dp", "graph"), None), P(("dp", "graph"), None), P(), P(), P(), P(),
            P(("dp", "graph"), None, None), P(("dp", "graph")), P(("dp", "graph")), P(("dp", "graph")),
        ),
        out_specs=(P(("dp", "graph"), None), P(), P(), P(), P()),
        check_vma=False,
    )
```
